32 devices in a mesh: sector: 8 (over z, y), mpo: 4 (over x, core).
Axes of the slice: x: 2, y: 2, z: 4, core: 2. Of those that a mesh axis runs over, the one named last changes fastest.
Arguments:
- psi: bfloat16 [16, 128, 2048], P('sector', 'mpo'), may hold values from -150 to 150
- left_env: bfloat16 [16, 128, 128, 128], P('sector', 'mpo'), may hold values from -0.5 to 0.5
- right_env: bfloat16 [16, 128, 128, 128], P('sector', 'mpo'), may hold values from -0.046875 to 0.046875
- term_op: int32 [128], P('mpo'), may hold values from 0 to 7
- ops: bfloat16 [8, 16, 16], replicated, may hold values from -1.5 to 1.5
- energy: float32 [16], replicated, may hold values from -2 to 2
- charge: int32 [16], P('sector'), may hold values from 0 to 15
- block_dims: int32 [16, 2], P('sector'), may hold values from 64 to 128, as said below
- basis: float32 [3, 16, 128, 2048], P(None, 'sector', 'mpo'), may hold values from -0.0029296875 to 0.0029296875
Outputs:
- hpsi: float32 [16, 128, 2048], P('sector', 'mpo')
- correction: float32 [16, 128, 2048], P('sector', 'mpo')
- ritz: float32 [], replicated
- subspace_row: float32 [3], replicated
The draws below stay inside these ranges and needn't reach their ends.
Inputs may be any that keep to these rules, and one draw needn't show every extreme that they name: block_dims[s, 0] rows and block_dims[s, 1] columns of each padded block are valid; some block is full.
All inputs are finite; a program needn't handle non-finite values.
Results may differ from the reference program's by a relative error of at most 0.002.
Values may be sent and summed in bfloat16 or wider, within the bound.
A program may use at most 64 MiB of HBM per device.

```python
import math
import jax
import jax.numpy as jnp
from jax import lax

BLK = 128
P_SIZE = 16
NOPS = 8
NCHARGE = 16
NB = 3
NSEC = 16
K = 128


def draw_psi(key, part):
    keys = jax.random.split(key, 3)
    width = P_SIZE * BLK
    block_pos = jnp.arange(NSEC, dtype=jnp.float32) / max(NSEC - 1, 1)
    block_scale = jnp.exp(jnp.log(3.0) * block_pos)[:, None, None]
    row_scale = jnp.exp(jax.random.uniform(keys[1], (NSEC, BLK, 1), jnp.float32, jnp.log(0.3), jnp.log(3.0)))
    col_scale = jnp.exp(jax.random.uniform(keys[2], (NSEC, 1, width), jnp.float32, jnp.log(0.3), jnp.log(3.0)))
    base = jnp.clip(jax.random.normal(keys[0], (NSEC, BLK, width), jnp.float32), -4.0, 4.0)
    values = base * block_scale * row_scale * col_scale
    return values.astype(jnp.bfloat16)


def draw_block_dims(key, part):
    dims = jax.random.randint(jax.random.fold_in(key, 11), (NSEC, 2), BLK // 2, BLK + 1, dtype=jnp.int32)
    full_at = jax.random.randint(jax.random.fold_in(key, 12), (), 0, NSEC, dtype=jnp.int32)
    least_at = jax.random.randint(jax.random.fold_in(key, 13), (), 0, NSEC, dtype=jnp.int32)
    dims = dims.at[least_at].set(BLK // 2)
    return dims.at[full_at].set(BLK)


def with_ends(result, key, low, largest):
    shape = result.shape
    spot = [jax.random.randint(jax.random.fold_in(key, axis), (), 0, shape[axis]) for axis in range(len(shape))]
    result = result.at[tuple(spot)].set(low)
    longest = shape.index(max(shape))
    spot[longest] = (spot[longest] + 1) % shape[longest]
    return result.at[tuple(spot)].set(largest)


def level_of(own_key, extent, pieces, low, high):
    gain = 1.0
    for axis_at, parts in pieces:
        draws = jax.random.uniform(jax.random.fold_in(jax.random.fold_in(own_key, 6), axis_at), (parts,), jnp.float32, low / len(pieces), high / len(pieces))
        gain = gain * jnp.repeat(jnp.exp(draws), extent[axis_at] // parts).reshape((-1,) + (1,) * (len(extent) - 1 - axis_at))
    return gain


def gaussian(own_key, shape, spread, limit, cuts=(), held_as=jnp.bfloat16):
    loudness = level_of(own_key, shape, cuts, -0.22, 0.18) if cuts else 1.0
    entries = jax.random.normal(own_key, shape, jnp.float32) * spread * loudness
    return jnp.minimum(jnp.maximum(entries, -limit), limit).astype(held_as)


def setup_inputs(seed: int = 0) -> dict:
    key_of = jax.random.split(jax.random.key(seed), 10)
    return {
        "psi": draw_psi(jax.random.fold_in(key_of[9], 71), 0),
        "left_env": gaussian(key_of[1], (NSEC, K, BLK, BLK), BLK ** -0.5, 0.5, ((0, 8), (1, 4))),
        "right_env": gaussian(key_of[2], (NSEC, K, BLK, BLK), (BLK * K) ** -0.5, 0.046875, ((0, 8), (1, 4))),
        "term_op": with_ends(jax.random.randint(key_of[3], (K,), 0, NOPS), jax.random.fold_in(key_of[3], 1), 0, NOPS - 1).astype(jnp.int32),
        "ops": gaussian(key_of[4], (NOPS, P_SIZE, P_SIZE), P_SIZE ** -0.5, 1.5),
        "energy": jnp.clip(jax.random.uniform(key_of[5], (NCHARGE,), jnp.float32, -2.0, 2.0), -2.0, 2.0),
        "charge": with_ends(jax.random.randint(key_of[6], (NSEC,), 0, NCHARGE), jax.random.fold_in(key_of[6], 1), 0, NCHARGE - 1).astype(jnp.int32),
        "block_dims": draw_block_dims(jax.random.fold_in(key_of[9], 71), 0),
        "basis": gaussian(key_of[8], (NB, NSEC, BLK, P_SIZE * BLK), (1.0 / (NSEC * BLK * P_SIZE * BLK) ** 0.5), 0.0029296875, ((1, 8), (2, 4)), jnp.float32),
    }


def sector_mask(block_dims, row_first, row_total, block_size, width):
    rows_ok = (row_first + jnp.arange(row_total, dtype=jnp.int32))[None, :, None] < block_dims[:, 0][:, None, None]
    cols_ok = (jnp.arange(width, dtype=jnp.int32) % block_size)[None, None, :] < block_dims[:, 1][:, None, None]
    return rows_ok & cols_ok

def reference(psi, left_env, right_env, term_op, ops, energy, charge, block_dims, basis):
    width = P_SIZE * BLK
    mask = sector_mask(block_dims, 0, BLK, BLK, width)
    masked = jnp.where(mask, psi, jnp.zeros_like(psi))
    op_mats = ops[term_op]
    level = energy[charge]
    group = math.gcd(K, 4)

    def per_block(items):
        block_x, block_left, block_right = items
        block_f = block_x.astype(jnp.float32)

        def one_group(running, offset):
            left_part = lax.dynamic_slice_in_dim(block_left, offset, group, 0).astype(jnp.float32)
            right_part = lax.dynamic_slice_in_dim(block_right, offset, group, 0).astype(jnp.float32)
            op_part = lax.dynamic_slice_in_dim(op_mats, offset, group, 0).astype(jnp.float32)
            moved = jnp.einsum('kac,cq->kaq', left_part, block_f).astype(jnp.bfloat16)
            moved = moved.astype(jnp.float32).reshape(group, BLK, P_SIZE, BLK)
            mixed = jnp.einsum('kpq,kaqb->kapb', op_part, moved).astype(jnp.bfloat16)
            running = running + jnp.einsum('kapc,kcb->apb', mixed.astype(jnp.float32), right_part)
            return (running, None)
        offsets = jnp.arange(K // group, dtype=jnp.int32) * group
        running, _ = lax.scan(one_group, jnp.zeros((BLK, P_SIZE, BLK), jnp.float32), offsets)
        return running.reshape(BLK, width)
    core = lax.map(per_block, (masked, left_env, right_env))
    masked_f = masked.astype(jnp.float32)
    hpsi = jnp.where(mask, level[:, None, None] * masked_f + core, jnp.zeros_like(core))
    self_sq = jnp.sum(masked_f * masked_f)
    cross = jnp.sum(masked_f * hpsi)
    ritz = cross / (self_sq + 1e-06)
    subspace_row = lax.optimization_barrier(jnp.sum(basis * hpsi[None], axis=(1, 2, 3)))
    resid = hpsi - ritz * masked_f
    resid_sq = jnp.sum(resid * resid)
    correction = resid / jnp.sqrt(resid_sq / (NSEC * BLK * P_SIZE * BLK) + 1e-06)
    return (hpsi, correction, ritz, subspace_row)
```

```python
import functools

import jax
import jax.numpy as jnp
from jax import lax
from jax.experimental import pallas as pl
from jax.experimental.pallas import tpu as pltpu
from jax.sharding import PartitionSpec as P

MESH = pl.DeviceIdType.MESH


def gather_kernel(n, sectors, psi_ref, out_ref, own_sem, send, recv, fsend, frecv):
    row = lax.axis_index("sector")
    me = lax.axis_index("mpo")
    chips = n // 2
    core, chip = lax.rem(me, 2), lax.div(me, 2)
    sib = chip * 2 + 1 - core

    def at(hop):
        return lax.rem(chip + hop, chips) * 2

    barrier = pltpu.get_barrier_semaphore()
    for hop in range(1, chips):
        pl.semaphore_signal(barrier, inc=1, device_id=(row, at(hop) + core), device_id_type=MESH)
    pl.semaphore_signal(barrier, inc=1, device_id=(row, sib), device_id_type=MESH)
    pl.semaphore_wait(barrier, chips)

    def push(src, block, s, to, ssem, rsem):
        return pltpu.make_async_remote_copy(
            src_ref=src,
            dst_ref=out_ref.at[block, s],
            send_sem=ssem,
            recv_sem=rsem,
            device_id=(row, to),
            device_id_type=MESH,
        )

    far, near, relay = {}, {}, {}
    for s in range(sectors):
        for hop in range(1, chips):
            far[hop, s] = push(
                psi_ref.at[s], me, s, at(hop) + core, send.at[hop, s], recv.at[hop, s]
            )
            far[hop, s].start()
    for s in range(sectors):
        near[s] = push(psi_ref.at[s], me, s, sib, send.at[0, s], recv.at[0, s])
        near[s].start()
    own = pltpu.make_async_copy(psi_ref, out_ref.at[me], own_sem)
    own.start()
    for s in range(sectors):
        for hop in range(1, chips):
            far[hop, s].wait_recv()
            block = at(chips - hop) + core
            relay[hop, s] = push(
                out_ref.at[block, s], block, s, sib, fsend.at[hop, s], frecv.at[hop, s]
            )
            relay[hop, s].start()
    own.wait()
    for s in range(sectors):
        near[s].wait()
        for hop in range(1, chips):
            far[hop, s].wait_send()
            relay[hop, s].wait()


def gather(psi, n):
    sectors, rows, width = psi.shape
    chips = n // 2
    return pl.pallas_call(
        functools.partial(gather_kernel, n, sectors),
        out_shape=jax.ShapeDtypeStruct((n, sectors, rows, width), psi.dtype),
        in_specs=[pl.BlockSpec(memory_space=pl.ANY)],
        out_specs=pl.BlockSpec(memory_space=pl.ANY),
        scratch_shapes=[pltpu.SemaphoreType.DMA(())]
        + [pltpu.SemaphoreType.DMA((chips, sectors))] * 4,
        compiler_params=pltpu.CompilerParams(collective_id=0, has_side_effects=True),
        name="gather",
    )(psi)


def terms_kernel(
    size_p, op_ref, opmat_ref, x_ref, left_ref, right_ref, out_ref, sums, count, first, lists
):
    terms = left_ref.shape[1]
    blk = left_ref.shape[2]
    op_count = count.shape[0]
    slots = lists.shape[1]

    for o in range(op_count):
        count[o] = 0

    def tally(k, c):
        o = op_ref[k]
        count[o] = count[o] + 1
        return c

    lax.fori_loop(0, terms, tally, 0)
    total = jnp.int32(0)
    for o in range(op_count):
        first[o] = total * 2
        total = total + lax.div(count[o] + 1, 2)

    def clear(i, c):
        lists[0, i] = 0
        lists[1, i] = 0
        lists[2, i] = 0
        return c

    lax.fori_loop(0, slots, clear, 0)

    def place(k, c):
        o = op_ref[k]
        spot = first[o]
        first[o] = spot + 1
        lists[0, spot] = k
        lists[1, spot] = 1
        lists[2, lax.div(spot, 2)] = o
        return c

    lax.fori_loop(0, terms, place, 0)

    sums[...] = jnp.zeros_like(sums)

    def pair(i, c):
        k1, k2 = lists[0, 2 * i], lists[0, 2 * i + 1]
        used = lists[1, 2 * i + 1]
        o = lists[2, i]
        left = jnp.concatenate([left_ref[0, k1], left_ref[0, k2]], axis=0)
        second = right_ref[0, k2]
        second = jnp.where(used > 0, second, jnp.zeros_like(second))
        right = jnp.concatenate([right_ref[0, k1], second], axis=0)
        step = 2
        for t in range(size_p // step):
            cols = pl.ds(t * step * blk, step * blk)
            v = jnp.dot(left, x_ref[0, :, cols], preferred_element_type=jnp.float32)
            v = v.astype(jnp.bfloat16)
            both = [
                jnp.concatenate(
                    [v[:blk, u * blk : (u + 1) * blk], v[blk:, u * blk : (u + 1) * blk]], axis=1
                )
                for u in range(step)
            ]
            both = jnp.concatenate(both, axis=0)
            start = pl.multiple_of(o * size_p * blk, blk) + t * step * blk
            rows = pl.ds(pl.multiple_of(start, blk), step * blk)
            sums[rows, :] = sums[rows, :] + jnp.dot(
                both, right, preferred_element_type=jnp.float32
            )
        return c

    lax.fori_loop(0, total, pair, 0)

    opmat = opmat_ref[...]
    depth = op_count * size_p

    def mix(i, c):
        for u in range(4):
            a = i * 8 + u * 2
            y = jnp.concatenate(
                [sums[pl.ds(a, depth, stride=blk), :], sums[pl.ds(a + 1, depth, stride=blk), :]],
                axis=1,
            )
            high = y.astype(jnp.bfloat16)
            low = (y - high.astype(jnp.float32)).astype(jnp.bfloat16)
            m = jnp.dot(
                opmat,
                jnp.concatenate([high, low], axis=0),
                preferred_element_type=jnp.float32,
            )
            base = pl.multiple_of(i * 8 * size_p, size_p) + u * 2 * size_p
            base = pl.multiple_of(base, size_p)
            out_ref[0, pl.ds(base, size_p), :] = m[:, :blk]
            out_ref[0, pl.ds(pl.multiple_of(base + size_p, size_p), size_p), :] = m[:, blk:]
        return c

    lax.fori_loop(0, blk // 8, mix, 0)


def local_terms(x, left, right, term_op, ops):
    sectors, terms, blk, _ = left.shape
    op_count, size_p, _ = ops.shape
    width = x.shape[2]
    opmat = jnp.transpose(ops, (1, 0, 2)).reshape(size_p, op_count * size_p)
    opmat = jnp.concatenate([opmat, opmat], axis=1)
    flops = 4 * sectors * terms * blk * blk * width
    return pl.pallas_call(
        functools.partial(terms_kernel, size_p),
        out_shape=jax.ShapeDtypeStruct((sectors, blk * size_p, blk), jnp.float32),
        grid=(sectors,),
        in_specs=[
            pl.BlockSpec(memory_space=pltpu.SMEM),
            pl.BlockSpec(opmat.shape, lambda s: (0, 0)),
            pl.BlockSpec((1, blk, width), lambda s: (s, 0, 0)),
            pl.BlockSpec((1, terms, blk, blk), lambda s: (s, 0, 0, 0)),
            pl.BlockSpec((1, terms, blk, blk), lambda s: (s, 0, 0, 0)),
        ],
        out_specs=pl.BlockSpec((1, blk * size_p, blk), lambda s: (s, 0, 0)),
        scratch_shapes=[
            pltpu.VMEM((op_count * size_p * blk, blk), jnp.float32),
            pltpu.SMEM((op_count,), jnp.int32),
            pltpu.SMEM((op_count,), jnp.int32),
            pltpu.SMEM((3, terms + op_count + 2), jnp.int32),
        ],
        compiler_params=pltpu.CompilerParams(vmem_limit_bytes=44 * 2**20),
        cost_estimate=pl.CostEstimate(
            flops=flops, bytes_accessed=4 * sectors * terms * blk * blk, transcendentals=0
        ),
        name="terms",
    )(term_op, opmat, x, left, right)


def merge(stats, nb):
    xx, xh = stats[:, 0:1], stats[:, 1:2]
    rr, xr = stats[:, 2 + nb : 3 + nb], stats[:, 3 + nb : 4 + nb]
    q = xh / (xx + 1e-6)
    total = jnp.sum(stats, axis=0)
    all_q = total[1:2] / (total[0:1] + 1e-6)
    gap = q - all_q[None]
    rr = jnp.sum(rr + 2.0 * gap * xr + gap * gap * xx, axis=0)
    xr = jnp.sum(xr + gap * xx, axis=0)
    return jnp.concatenate(
        [total[: 2 + nb], rr, xr, jnp.zeros((4 - nb, total.shape[1]), jnp.float32)], axis=0
    ), all_q


def finish_kernel(
    n,
    groups,
    cells,
    dims_ref,
    level_ref,
    part_ref,
    psi_ref,
    basis_hbm,
    hpsi_ref,
    corr_ref,
    stat_ref,
    basis_ref,
    mine,
    theirs,
    landed,
    slots_m,
    slots_s,
    tile,
    basis_sem,
    load_sem,
    send1,
    recv1,
    send2,
    recv2,
    send3,
    recv3,
):
    row = lax.axis_index("sector")
    me = lax.axis_index("mpo")
    chips = n // 2
    core, chip = lax.rem(me, 2), lax.div(me, 2)
    sib = chip * 2 + 1 - core
    sectors, rows, width = psi_ref.shape
    nb = basis_ref.shape[0]
    blk = part_ref.shape[2]
    size_p = width // blk
    chunk = rows * size_p

    barrier = pltpu.get_barrier_semaphore()
    for j in range(1, n):
        pl.semaphore_signal(
            barrier, inc=1, device_id=(row, lax.rem(me + j, n)), device_id_type=MESH
        )
    for j in range(1, groups):
        pl.semaphore_signal(
            barrier, inc=1, device_id=(lax.rem(row + j, groups), me), device_id_type=MESH
        )
    basis_copy = pltpu.make_async_copy(basis_hbm, basis_ref, basis_sem)
    pl.semaphore_wait(barrier, n + groups - 2)

    def part(hop, which, s):
        block = lax.rem(chip + hop, chips) * 2 + which
        return part_ref.at[s, pl.ds(pl.multiple_of(block * chunk, chunk), chunk)]

    order = list(range(1, chips)) + [0]
    loads, swaps, sends = {}, {}, {}
    for hop in order:
        for s in range(sectors):
            swaps[hop, s] = pltpu.make_async_remote_copy(
                src_ref=part(hop, 1 - core, s),
                dst_ref=theirs.at[hop, s],
                send_sem=send1.at[hop, s],
                recv_sem=recv1.at[hop, s],
                device_id=(row, sib),
                device_id_type=MESH,
            )
            swaps[hop, s].start()
            loads[hop, s] = pltpu.make_async_copy(
                part(hop, core, s), mine.at[hop, s], load_sem.at[hop, s]
            )
            loads[hop, s].start()
    basis_copy.start()
    for hop in order:
        for s in range(sectors):
            loads[hop, s].wait()
            swaps[hop, s].wait_recv()
            mine[hop, s] = mine[hop, s] + theirs[hop, s]
            if hop:
                sends[hop, s] = pltpu.make_async_remote_copy(
                    src_ref=mine.at[hop, s],
                    dst_ref=landed.at[hop - 1, s],
                    send_sem=send2.at[hop, s],
                    recv_sem=recv2.at[hop, s],
                    device_id=(row, lax.rem(chip + hop, chips) * 2 + core),
                    device_id_type=MESH,
                )
                sends[hop, s].start()
    basis_copy.wait()

    row_at = me * rows + lax.broadcasted_iota(jnp.int32, (rows, blk), 0)
    col_at = lax.broadcasted_iota(jnp.int32, (rows, blk), 1)
    zero = jnp.zeros((rows, blk), jnp.float32)
    xx, xh, bh = zero, zero, [zero] * nb
    for s in range(sectors):
        for hop in range(1, chips):
            sends[hop, s].wait_recv()
        mask = (row_at < dims_ref[s, 0]) & (col_at < dims_ref[s, 1])
        level = level_ref[s]
        for p in range(size_p):
            cols = slice(p * blk, (p + 1) * blk)
            spots = pl.ds(p, rows, stride=size_p)
            core_p = mine[0, s, spots, :]
            for hop in range(1, chips):
                core_p = core_p + landed[hop - 1, s, spots, :]
            x = jnp.where(mask, psi_ref[s, :, cols].astype(jnp.float32), zero)
            h = jnp.where(mask, level * x + core_p, zero)
            hpsi_ref[s, :, cols] = h
            corr_ref[s, :, cols] = x
            xx = xx + x * x
            xh = xh + x * h
            bh = [bh[j] + basis_ref[j, s, :, cols] * h for j in range(nb)]

    def whole(v):
        v = jnp.sum(jnp.sum(v, axis=0, keepdims=True), axis=1, keepdims=True)
        return jnp.broadcast_to(v, (1, blk))

    xx, xh, bh = whole(xx), whole(xh), [whole(b) for b in bh]
    q = xh / (xx + 1e-6)
    rr, xr = zero, zero
    for s in range(sectors):
        for p in range(size_p):
            cols = slice(p * blk, (p + 1) * blk)
            x = corr_ref[s, :, cols]
            r = hpsi_ref[s, :, cols] - q * x
            rr = rr + r * r
            xr = xr + x * r
    stats = jnp.concatenate(
        [xx, xh] + bh + [whole(rr), whole(xr), jnp.zeros((4 - nb, blk), jnp.float32)], axis=0
    )

    def spread(level_no, stats, slots, count, mine_at, target):
        tile[level_no] = stats
        slots[mine_at] = stats
        for j in range(1, count):
            pltpu.make_async_remote_copy(
                src_ref=tile.at[level_no],
                dst_ref=slots.at[mine_at],
                send_sem=send3.at[level_no],
                recv_sem=recv3.at[level_no],
                device_id=target(j),
                device_id_type=MESH,
            ).start()
        some = slots.at[pl.ds(0, count - 1)]
        pltpu.make_async_copy(some, some, recv3.at[level_no]).wait()
        pltpu.make_async_copy(some, some, send3.at[level_no]).wait()
        return merge(slots[...], nb)

    stats, q = spread(0, stats, slots_m, n, me, lambda j: (row, lax.rem(me + j, n)))
    stats, q = spread(1, stats, slots_s, groups, row, lambda j: (lax.rem(row + j, groups), me))
    stat_ref[...] = jnp.concatenate([q, stats[1:]], axis=0)
    scale = 1.0 / jnp.sqrt(stats[2 + nb : 3 + nb] / cells + 1e-6)
    for s in range(sectors):
        for p in range(size_p):
            cols = slice(p * blk, (p + 1) * blk)
            corr_ref[s, :, cols] = (hpsi_ref[s, :, cols] - q * corr_ref[s, :, cols]) * scale
    for s in range(sectors):
        for hop in order:
            swaps[hop, s].wait_send()
            if hop:
                sends[hop, s].wait_send()


def finish(parts, psi, basis, dims, level, n, groups):
    sectors, rows, width = psi.shape
    nb = basis.shape[0]
    blk = parts.shape[2]
    chips = n // 2
    chunk = rows * (width // blk)
    cells = float(sectors * groups * rows * n * width)
    smem = pl.BlockSpec(memory_space=pltpu.SMEM)
    vmem = pl.BlockSpec(memory_space=pltpu.VMEM)
    far = pl.BlockSpec(memory_space=pl.ANY)
    dma = pltpu.SemaphoreType.DMA
    like = jax.ShapeDtypeStruct(psi.shape, jnp.float32)
    return pl.pallas_call(
        functools.partial(finish_kernel, n, groups, cells),
        out_shape=(like, like, jax.ShapeDtypeStruct((8, blk), jnp.float32)),
        in_specs=[smem, smem, far, vmem, far],
        out_specs=(vmem, vmem, vmem),
        scratch_shapes=[
            pltpu.VMEM(basis.shape, jnp.float32),
            pltpu.VMEM((chips, sectors, chunk, blk), jnp.float32),
            pltpu.VMEM((chips, sectors, chunk, blk), jnp.float32),
            pltpu.VMEM((max(chips - 1, 1), sectors, chunk, blk), jnp.float32),
            pltpu.VMEM((n, 8, blk), jnp.float32),
            pltpu.VMEM((groups, 8, blk), jnp.float32),
            pltpu.VMEM((2, 8, blk), jnp.float32),
            dma(()),
            dma((chips, sectors)),
            dma((chips, sectors)),
            dma((chips, sectors)),
            dma((chips, sectors)),
            dma((chips, sectors)),
            dma((2,)),
            dma((2,)),
        ],
        compiler_params=pltpu.CompilerParams(
            collective_id=1, has_side_effects=True, vmem_limit_bytes=32 * 2**20
        ),
        name="finish",
    )(dims, level, parts, psi, basis)


def body(n, groups, psi, left_env, right_env, term_op, ops, energy, charge, block_dims, basis):
    blk = left_env.shape[-1]
    sectors, rows, width = psi.shape
    x = jnp.transpose(gather(psi, n), (1, 0, 2, 3)).reshape(sectors, n * rows, width)
    rows_ok = jnp.arange(blk, dtype=jnp.int32)[None, :, None] < block_dims[:, 0][:, None, None]
    cols_ok = (jnp.arange(width, dtype=jnp.int32) % blk)[None, None, :] < block_dims[:, 1][
        :, None, None
    ]
    x = jnp.where(rows_ok & cols_ok, x, jnp.zeros_like(x))
    parts = local_terms(x, left_env, right_env, term_op, ops)
    hot = (charge[:, None] == jnp.arange(energy.shape[0], dtype=jnp.int32)[None, :]).astype(
        jnp.float32
    )
    level = jnp.sum(hot * energy[None, :], axis=1)
    hpsi, correction, stats = finish(parts, psi, basis, block_dims, level, n, groups)
    return (hpsi, correction, stats[0, 0], stats[2 : 2 + basis.shape[0], 0])


def solution(mesh):
    placed = (
        P("sector", "mpo", None),
        P("sector", "mpo", None, None),
        P("sector", "mpo", None, None),
        P("mpo"),
        P(),
        P(),
        P("sector"),
        P("sector", None),
        P(None, "sector", "mpo", None),
    )
    return jax.shard_map(
        functools.partial(body, mesh.shape["mpo"], mesh.shape["sector"]),
        mesh=mesh,
        in_specs=placed,
        out_specs=(P("sector", "mpo", None), P("sector", "mpo", None), P(), P()),
        check_vma=False,
    )
```

```python
import functools

import jax
import jax.numpy as jnp
from jax import lax
from jax.experimental import pallas as pl
from jax.experimental.pallas import tpu as pltpu
from jax.sharding import PartitionSpec as P

MESH = pl.DeviceIdType.MESH


def gather_kernel(n, sectors, flat, psi_ref, out_ref, own_sem, send, recv, fsend, frecv):
    row = lax.axis_index("sector")
    me = lax.axis_index("mpo")
    chips = n // 2
    core, chip = lax.rem(me, 2), lax.div(me, 2)
    sib = chip * 2 + 1 - core

    rows = psi_ref.shape[1]

    def at(hop):
        return lax.rem(chip + hop, chips) * 2

    def slot(block, s):
        if flat:
            return out_ref.at[s, pl.ds(pl.multiple_of(block * rows, rows), rows)]
        return out_ref.at[block, s]

    barrier = pltpu.get_barrier_semaphore()
    for hop in range(1, chips):
        pl.semaphore_signal(barrier, inc=1, device_id=(row, at(hop) + core), device_id_type=MESH)
    pl.semaphore_signal(barrier, inc=1, device_id=(row, sib), device_id_type=MESH)
    pl.semaphore_wait(barrier, chips)

    def push(src, block, s, to, ssem, rsem):
        return pltpu.make_async_remote_copy(
            src_ref=src,
            dst_ref=slot(block, s),
            send_sem=ssem,
            recv_sem=rsem,
            device_id=(row, to),
            device_id_type=MESH,
        )

    far, near, relay = {}, {}, {}
    for s in range(sectors):
        for hop in range(1, chips):
            far[hop, s] = push(
                psi_ref.at[s], me, s, at(hop) + core, send.at[hop, s], recv.at[hop, s]
            )
            far[hop, s].start()
    for s in range(sectors):
        near[s] = push(psi_ref.at[s], me, s, sib, send.at[0, s], recv.at[0, s])
        near[s].start()
    own = [
        pltpu.make_async_copy(psi_ref.at[s], slot(me, s), own_sem.at[s]) for s in range(sectors)
    ]
    for copy in own:
        copy.start()
    for s in range(sectors):
        for hop in range(1, chips):
            far[hop, s].wait_recv()
            block = at(chips - hop) + core
            relay[hop, s] = push(
                slot(block, s), block, s, sib, fsend.at[hop, s], frecv.at[hop, s]
            )
            relay[hop, s].start()
    for s in range(sectors):
        own[s].wait()
        near[s].wait()
        for hop in range(1, chips):
            far[hop, s].wait_send()
            relay[hop, s].wait()


def gather(psi, n):
    sectors, rows, width = psi.shape
    chips = n // 2
    flat = rows % 16 == 0
    shape = (sectors, n * rows, width) if flat else (n, sectors, rows, width)
    out = pl.pallas_call(
        functools.partial(gather_kernel, n, sectors, flat),
        out_shape=jax.ShapeDtypeStruct(shape, psi.dtype),
        in_specs=[pl.BlockSpec(memory_space=pl.ANY)],
        out_specs=pl.BlockSpec(memory_space=pl.ANY),
        scratch_shapes=[pltpu.SemaphoreType.DMA((sectors,))]
        + [pltpu.SemaphoreType.DMA((chips, sectors))] * 4,
        compiler_params=pltpu.CompilerParams(collective_id=0, has_side_effects=True),
        name="gather",
    )(psi)
    if flat:
        return out
    return jnp.transpose(out, (1, 0, 2, 3)).reshape(sectors, n * rows, width)


def terms_kernel(
    size_p, op_ref, opmat_ref, x_ref, left_ref, right_ref, out_ref, sums, count, first, lists
):
    terms = left_ref.shape[1]
    blk = left_ref.shape[2]
    op_count = count.shape[0]
    slots = lists.shape[1]
    pitch = sums.shape[1] // size_p

    for o in range(op_count):
        count[o] = 0

    def tally(k, c):
        o = op_ref[k]
        count[o] = count[o] + 1
        return c

    lax.fori_loop(0, terms, tally, 0)
    total = jnp.int32(0)
    for o in range(op_count):
        first[o] = total * 2
        total = total + lax.div(count[o] + 1, 2)

    def clear(i, c):
        lists[0, i] = 0
        lists[1, i] = 0
        lists[2, i] = 0
        return c

    lax.fori_loop(0, slots, clear, 0)

    def place(k, c):
        o = op_ref[k]
        spot = first[o]
        first[o] = spot + 1
        lists[0, spot] = k
        lists[1, spot] = 1
        lists[2, lax.div(spot, 2)] = o
        return c

    lax.fori_loop(0, terms, place, 0)

    sums[...] = jnp.zeros_like(sums)

    def pairs(i, c):
        lefts, rights, ops_at = [], [], []
        for at in (2 * i, 2 * i + 1):
            k1, k2 = lists[0, 2 * at], lists[0, 2 * at + 1]
            lefts += [left_ref[0, k1], left_ref[0, k2]]
            r1, r2 = right_ref[0, k1], right_ref[0, k2]
            r1 = jnp.where(lists[1, 2 * at] > 0, r1, jnp.zeros_like(r1))
            r2 = jnp.where(lists[1, 2 * at + 1] > 0, r2, jnp.zeros_like(r2))
            rights.append(jnp.concatenate([r1, r2], axis=0))
            ops_at.append(lists[2, at])
        v = jnp.dot(
            jnp.concatenate(lefts, axis=0), x_ref[0], preferred_element_type=jnp.float32
        ).astype(jnp.bfloat16)
        for j in range(2):
            w = v[2 * j * blk : 2 * (j + 1) * blk]
            both = [
                jnp.concatenate(
                    [w[:blk, p * blk : (p + 1) * blk], w[blk:, p * blk : (p + 1) * blk]], axis=1
                )
                for p in range(size_p)
            ]
            m = jnp.dot(
                jnp.concatenate(both, axis=0), rights[j], preferred_element_type=jnp.float32
            )
            for p in range(size_p):
                rows = pl.ds(p * pitch, blk)
                sums[ops_at[j], rows, :] = sums[ops_at[j], rows, :] + m[p * blk : (p + 1) * blk]
        return c

    lax.fori_loop(0, lax.div(total + 1, 2), pairs, 0)

    flat = sums.reshape(op_count * size_p * pitch, blk)
    opmat = opmat_ref[...]
    depth = op_count * size_p

    def mix(i, c):
        for u in range(4):
            a = i * 8 + u * 2
            y = jnp.concatenate(
                [flat[pl.ds(a, depth, stride=pitch), :], flat[pl.ds(a + 1, depth, stride=pitch), :]],
                axis=1,
            )
            high = y.astype(jnp.bfloat16)
            low = (y - high.astype(jnp.float32)).astype(jnp.bfloat16)
            m = jnp.dot(
                opmat,
                jnp.concatenate([high, low], axis=0),
                preferred_element_type=jnp.float32,
            )
            base = pl.multiple_of(i * 8 * size_p, size_p) + u * 2 * size_p
            base = pl.multiple_of(base, size_p)
            out_ref[0, pl.ds(base, size_p), :] = m[:, :blk]
            out_ref[0, pl.ds(pl.multiple_of(base + size_p, size_p), size_p), :] = m[:, blk:]
        return c

    lax.fori_loop(0, blk // 8, mix, 0)


def local_terms(x, left, right, term_op, ops):
    sectors, terms, blk, _ = left.shape
    op_count, size_p, _ = ops.shape
    width = x.shape[2]
    opmat = jnp.transpose(ops, (1, 0, 2)).reshape(size_p, op_count * size_p)
    opmat = jnp.concatenate([opmat, opmat], axis=1)
    flops = 4 * sectors * terms * blk * blk * width
    return pl.pallas_call(
        functools.partial(terms_kernel, size_p),
        out_shape=jax.ShapeDtypeStruct((sectors, blk * size_p, blk), jnp.float32),
        grid=(sectors,),
        in_specs=[
            pl.BlockSpec(memory_space=pltpu.SMEM),
            pl.BlockSpec(opmat.shape, lambda s: (0, 0)),
            pl.BlockSpec((1, blk, width), lambda s: (s, 0, 0)),
            pl.BlockSpec((1, terms, blk, blk), lambda s: (s, 0, 0, 0)),
            pl.BlockSpec((1, terms, blk, blk), lambda s: (s, 0, 0, 0)),
        ],
        out_specs=pl.BlockSpec((1, blk * size_p, blk), lambda s: (s, 0, 0)),
        scratch_shapes=[
            pltpu.VMEM((op_count, size_p * (blk + 8), blk), jnp.float32),
            pltpu.SMEM((op_count,), jnp.int32),
            pltpu.SMEM((op_count,), jnp.int32),
            pltpu.SMEM((3, terms + op_count + 8), jnp.int32),
        ],
        compiler_params=pltpu.CompilerParams(vmem_limit_bytes=44 * 2**20),
        cost_estimate=pl.CostEstimate(
            flops=flops, bytes_accessed=4 * sectors * terms * blk * blk, transcendentals=0
        ),
        name="terms",
    )(term_op, opmat, x, left, right)


def merge(stats, nb):
    xx, xh = stats[:, 0:1], stats[:, 1:2]
    rr, xr = stats[:, 2 + nb : 3 + nb], stats[:, 3 + nb : 4 + nb]
    q = xh / (xx + 1e-6)
    total = jnp.sum(stats, axis=0)
    all_q = total[1:2] / (total[0:1] + 1e-6)
    gap = q - all_q[None]
    rr = jnp.sum(rr + 2.0 * gap * xr + gap * gap * xx, axis=0)
    xr = jnp.sum(xr + gap * xx, axis=0)
    return jnp.concatenate(
        [total[: 2 + nb], rr, xr, jnp.zeros((4 - nb, total.shape[1]), jnp.float32)], axis=0
    ), all_q


def finish_kernel(
    n,
    groups,
    cells,
    dims_ref,
    level_ref,
    part_ref,
    psi_ref,
    basis_hbm,
    hpsi_ref,
    corr_ref,
    stat_ref,
    basis_ref,
    mine,
    theirs,
    away,
    landed,
    slots_m,
    slots_s,
    tile,
    basis_sem,
    load_sem,
    send1,
    recv1,
    send2,
    recv2,
    send3,
    recv3,
):
    row = lax.axis_index("sector")
    me = lax.axis_index("mpo")
    chips = n // 2
    core, chip = lax.rem(me, 2), lax.div(me, 2)
    sib = chip * 2 + 1 - core
    sectors, rows, width = psi_ref.shape
    nb = basis_ref.shape[0]
    blk = part_ref.shape[2]
    size_p = width // blk
    chunk = rows * size_p

    barrier = pltpu.get_barrier_semaphore()
    for j in range(1, n):
        pl.semaphore_signal(
            barrier, inc=1, device_id=(row, lax.rem(me + j, n)), device_id_type=MESH
        )
    for j in range(1, groups):
        pl.semaphore_signal(
            barrier, inc=1, device_id=(lax.rem(row + j, groups), me), device_id_type=MESH
        )
    basis_copy = pltpu.make_async_copy(basis_hbm, basis_ref, basis_sem)
    pl.semaphore_wait(barrier, n + groups - 2)

    def part(hop, which, s):
        block = lax.rem(chip + hop, chips) * 2 + which
        return part_ref.at[s, pl.ds(pl.multiple_of(block * chunk, chunk), chunk)]

    order = list(range(1, chips)) + [0]
    loads, swaps, sends = {}, {}, {}
    for hop in order:
        for s in range(sectors):
            swaps[hop, s] = pltpu.make_async_remote_copy(
                src_ref=part(hop, 1 - core, s),
                dst_ref=theirs.at[hop, s],
                send_sem=send1.at[hop, s],
                recv_sem=recv1.at[hop, s],
                device_id=(row, sib),
                device_id_type=MESH,
            )
            swaps[hop, s].start()
            loads[hop, s] = pltpu.make_async_copy(
                part(hop, core, s), mine.at[hop, s], load_sem.at[hop, s]
            )
            loads[hop, s].start()
    basis_copy.start()
    for hop in order:
        for s in range(sectors):
            loads[hop, s].wait()
            swaps[hop, s].wait_recv()
            if hop == 0:
                mine[0, s] = mine[0, s] + theirs[0, s]
            else:
                away[hop - 1, s] = (mine[hop, s] + theirs[hop, s]).astype(jnp.bfloat16)
                sends[hop, s] = pltpu.make_async_remote_copy(
                    src_ref=away.at[hop - 1, s],
                    dst_ref=landed.at[hop - 1, s],
                    send_sem=send2.at[hop, s],
                    recv_sem=recv2.at[hop, s],
                    device_id=(row, lax.rem(chip + hop, chips) * 2 + core),
                    device_id_type=MESH,
                )
                sends[hop, s].start()
    basis_copy.wait()

    row_at = me * rows + lax.broadcasted_iota(jnp.int32, (rows, blk), 0)
    col_at = lax.broadcasted_iota(jnp.int32, (rows, blk), 1)
    zero = jnp.zeros((rows, blk), jnp.float32)
    xx, xh, bh = zero, zero, [zero] * nb
    for s in range(sectors):
        for hop in range(1, chips):
            sends[hop, s].wait_recv()
            mine[0, s] = mine[0, s] + landed[hop - 1, s].astype(jnp.float32)
        mask = (row_at < dims_ref[s, 0]) & (col_at < dims_ref[s, 1])
        level = level_ref[s]
        for p in range(size_p):
            cols = slice(p * blk, (p + 1) * blk)
            spots = pl.ds(p, rows, stride=size_p)
            core_p = mine[0, s, spots, :]
            x = jnp.where(mask, psi_ref[s, :, cols].astype(jnp.float32), zero)
            h = jnp.where(mask, level * x + core_p, zero)
            hpsi_ref[s, :, cols] = h
            corr_ref[s, :, cols] = x
            xx = xx + x * x
            xh = xh + x * h
            bh = [bh[j] + basis_ref[j, s, :, cols] * h for j in range(nb)]

    def whole(v):
        v = jnp.sum(jnp.sum(v, axis=0, keepdims=True), axis=1, keepdims=True)
        return jnp.broadcast_to(v, (1, blk))

    xx, xh, bh = whole(xx), whole(xh), [whole(b) for b in bh]
    q = xh / (xx + 1e-6)
    rr, xr = zero, zero
    for s in range(sectors):
        for p in range(size_p):
            cols = slice(p * blk, (p + 1) * blk)
            x = corr_ref[s, :, cols]
            r = hpsi_ref[s, :, cols] - q * x
            rr = rr + r * r
            xr = xr + x * r
    stats = jnp.concatenate(
        [xx, xh] + bh + [whole(rr), whole(xr), jnp.zeros((4 - nb, blk), jnp.float32)], axis=0
    )

    def spread(level_no, stats, slots, count, mine_at, target):
        tile[level_no] = stats
        slots[mine_at] = stats
        for j in range(1, count):
            pltpu.make_async_remote_copy(
                src_ref=tile.at[level_no],
                dst_ref=slots.at[mine_at],
                send_sem=send3.at[level_no],
                recv_sem=recv3.at[level_no],
                device_id=target(j),
                device_id_type=MESH,
            ).start()
        some = slots.at[pl.ds(0, count - 1)]
        pltpu.make_async_copy(some, some, recv3.at[level_no]).wait()
        pltpu.make_async_copy(some, some, send3.at[level_no]).wait()
        return merge(slots[...], nb)

    stats, q = spread(0, stats, slots_m, n, me, lambda j: (row, lax.rem(me + j, n)))
    stats, q = spread(1, stats, slots_s, groups, row, lambda j: (lax.rem(row + j, groups), me))
    stat_ref[...] = jnp.concatenate([q, stats[1:]], axis=0)
    scale = 1.0 / jnp.sqrt(stats[2 + nb : 3 + nb] / cells + 1e-6)
    for s in range(sectors):
        for p in range(size_p):
            cols = slice(p * blk, (p + 1) * blk)
            corr_ref[s, :, cols] = (hpsi_ref[s, :, cols] - q * corr_ref[s, :, cols]) * scale
    for s in range(sectors):
        for hop in order:
            swaps[hop, s].wait_send()
            if hop:
                sends[hop, s].wait_send()


def finish(parts, psi, basis, dims, level, n, groups):
    sectors, rows, width = psi.shape
    nb = basis.shape[0]
    blk = parts.shape[2]
    chips = n // 2
    chunk = rows * (width // blk)
    cells = float(sectors * groups * rows * n * width)
    smem = pl.BlockSpec(memory_space=pltpu.SMEM)
    vmem = pl.BlockSpec(memory_space=pltpu.VMEM)
    far = pl.BlockSpec(memory_space=pl.ANY)
    dma = pltpu.SemaphoreType.DMA
    like = jax.ShapeDtypeStruct(psi.shape, jnp.float32)
    return pl.pallas_call(
        functools.partial(finish_kernel, n, groups, cells),
        out_shape=(like, like, jax.ShapeDtypeStruct((8, blk), jnp.float32)),
        in_specs=[smem, smem, far, vmem, far],
        out_specs=(vmem, vmem, vmem),
        scratch_shapes=[
            pltpu.VMEM(basis.shape, jnp.float32),
            pltpu.VMEM((chips, sectors, chunk, blk), jnp.float32),
            pltpu.VMEM((chips, sectors, chunk, blk), jnp.float32),
            pltpu.VMEM((max(chips - 1, 1), sectors, chunk, blk), jnp.bfloat16),
            pltpu.VMEM((max(chips - 1, 1), sectors, chunk, blk), jnp.bfloat16),
            pltpu.VMEM((n, 8, blk), jnp.float32),
            pltpu.VMEM((groups, 8, blk), jnp.float32),
            pltpu.VMEM((2, 8, blk), jnp.float32),
            dma(()),
            dma((chips, sectors)),
            dma((chips, sectors)),
            dma((chips, sectors)),
            dma((chips, sectors)),
            dma((chips, sectors)),
            dma((2,)),
            dma((2,)),
        ],
        compiler_params=pltpu.CompilerParams(
            collective_id=1, has_side_effects=True, vmem_limit_bytes=32 * 2**20
        ),
        name="finish",
    )(dims, level, parts, psi, basis)


def body(n, groups, psi, left_env, right_env, term_op, ops, energy, charge, block_dims, basis):
    blk = left_env.shape[-1]
    sectors, rows, width = psi.shape
    x = gather(psi, n)
    rows_ok = jnp.arange(blk, dtype=jnp.int32)[None, :, None] < block_dims[:, 0][:, None, None]
    cols_ok = (jnp.arange(width, dtype=jnp.int32) % blk)[None, None, :] < block_dims[:, 1][
        :, None, None
    ]
    x = jnp.where(rows_ok & cols_ok, x, jnp.zeros_like(x))
    parts = local_terms(x, left_env, right_env, term_op, ops)
    hot = (charge[:, None] == jnp.arange(energy.shape[0], dtype=jnp.int32)[None, :]).astype(
        jnp.float32
    )
    level = jnp.sum(hot * energy[None, :], axis=1)
    hpsi, correction, stats = finish(parts, psi, basis, block_dims, level, n, groups)
    return (hpsi, correction, stats[0, 0], stats[2 : 2 + basis.shape[0], 0])


def solution(mesh):
    placed = (
        P("sector", "mpo", None),
        P("sector", "mpo", None, None),
        P("sector", "mpo", None, None),
        P("mpo"),
        P(),
        P(),
        P("sector"),
        P("sector", None),
        P(None, "sector", "mpo", None),
    )
    return jax.shard_map(
        functools.partial(body, mesh.shape["mpo"], mesh.shape["sector"]),
        mesh=mesh,
        in_specs=placed,
        out_specs=(P("sector", "mpo", None), P("sector", "mpo", None), P(), P()),
        check_vma=False,
    )
```
